32 devices in a mesh: section: 2 (over y), ctx: 16 (over z, x, core).
Axes of the slice: x: 2, y: 2, z: 4, core: 2. Of those that a mesh axis runs over, the one named last changes fastest.
Arguments:
- query_rows: bfloat16 [2, 2048, 896], P('section', 'ctx'), may hold values from -6 to 6
- key_rows: bfloat16 [2, 2048, 128], P('section', 'ctx'), may hold values from -6 to 6
- value_rows: bfloat16 [2, 2048, 128], P('section', 'ctx'), may hold values from -6 to 6
- attn_output: bfloat16 [2, 2048, 896], P('section', 'ctx'), may hold values from -6 to 6
- grad_output: bfloat16 [2, 2048, 896], P('section', 'ctx'), may hold values from -24 to 24
- log_normalizer: float32 [2, 7, 2048], P('section', None, 'ctx'), as said below
- positions: int32 [2048], P('ctx'), may hold values from 0 to 2047, as said below
Outputs:
- grad_query: bfloat16 [2, 2048, 896], P('section', 'ctx')
- grad_key: bfloat16 [2, 2048, 128], P('section', 'ctx')
- grad_value: bfloat16 [2, 2048, 128], P('section', 'ctx')
The draws below stay inside these ranges and needn't reach their ends.
Inputs may be any that keep to these rules, and one draw needn't show every extreme that they name: Each of 0 to 2047 appears once. The positions are cut into 32 runs of 64 consecutive positions; the rows of each device of ctx hold run r and then run 32 - 1 - r, each ascending, where which r a device holds is drawn, one device for each r. `log_normalizer`: within 0.5 of log(1 + the row's position) + 1.
All inputs are finite; a program needn't handle non-finite values.
Results may differ from the reference program's by a relative error of at most 0.0051.
Values may be sent and summed in bfloat16 or wider, within the bound.
A program may use at most 64 MiB of HBM per device.

```python
import math
import jax
import jax.numpy as jnp
from jax import lax

HD = 128
GROUP = 7
SECTIONS = 2
SEQ = 2048
HALF = 64
NRUNS = 32


def run_positions(key):
    order = jax.random.permutation(key, NRUNS // 2).astype(jnp.int32)
    offsets = jnp.arange(HALF, dtype=jnp.int32)
    first = order[:, None] * HALF + offsets[None, :]
    second = (NRUNS - 1 - order)[:, None] * HALF + offsets[None, :]
    return jnp.concatenate([first, second], axis=1).reshape(SEQ).astype(jnp.int32)


def draw_positions(key, part):
    rows_pos = run_positions(key)
    return rows_pos


def draw_log_normalizer(key, part):
    rows_pos = run_positions(key)
    key = jax.random.fold_in(key, 23)
    noise = jax.random.uniform(key, (SECTIONS, GROUP, SEQ), jnp.float32, -0.4, 0.4)
    base = jnp.log(1.0 + rows_pos.astype(jnp.float32)) + 1.0
    return base[None, None, :] + noise


def levels(rng, dims, shards, low, high):
    def one(axis_at, shards_of):
        steps = jax.random.uniform(jax.random.fold_in(jax.random.fold_in(rng, 6), axis_at), (shards_of,), jnp.float32, low / len(shards), high / len(shards))
        return jnp.repeat(jnp.exp(steps), dims[axis_at] // shards_of).reshape((-1,) + (1,) * (len(dims) - axis_at - 1))

    gain = one(*shards[0])
    for cut in shards[1:]:
        gain = gain * one(*cut)
    return gain


def scatter_about(rng, shape, deviation, reach, shards=(), kind=jnp.bfloat16):
    factor_of = levels(rng, shape, shards, -0.22, 0.18) if shards else 1.0
    result = jax.random.normal(rng, shape, jnp.float32) * deviation * factor_of
    return jnp.minimum(jnp.maximum(result, -reach), reach).astype(kind)


def setup_inputs(seed: int = 0) -> dict:
    splits = jax.random.split(jax.random.key(seed), 8)
    query_rows = scatter_about(splits[0], (SECTIONS, SEQ, GROUP * HD), 1.0, 6.0, ((0, 2), (1, 16)))
    key_rows = scatter_about(splits[1], (SECTIONS, SEQ, HD), 1.0, 6.0, ((0, 2), (1, 16)))
    value_rows = scatter_about(splits[2], (SECTIONS, SEQ, HD), 1.0, 6.0, ((0, 2), (1, 16)))
    attn_output = scatter_about(splits[3], (SECTIONS, SEQ, GROUP * HD), 1.0, 6.0, ((0, 2), (1, 16)))
    grad_output = scatter_about(splits[4], (SECTIONS, SEQ, GROUP * HD), 4.0, 24.0, ((0, 2), (1, 16)))
    log_normalizer = draw_log_normalizer(jax.random.fold_in(splits[7], 71), 0)
    positions = draw_positions(jax.random.fold_in(splits[7], 71), 0)
    return {"query_rows": query_rows, "key_rows": key_rows, "value_rows": value_rows, "attn_output": attn_output, "grad_output": grad_output, "log_normalizer": log_normalizer, "positions": positions}


def section_grads(query_rows, key_rows, value_rows, attn_output, grad_output, log_normalizer, positions):
    seq_len = query_rows.shape[0]
    scaling = HD ** -0.5
    row_block = math.gcd(seq_len, 256)
    query3 = query_rows.reshape(seq_len, GROUP, HD).astype(jnp.float32)
    grad3 = grad_output.reshape(seq_len, GROUP, HD).astype(jnp.float32)
    out3 = attn_output.reshape(seq_len, GROUP, HD).astype(jnp.float32)
    grad_dot = jnp.sum(grad3 * out3, axis=2).T
    key_full = key_rows.astype(jnp.float32)
    value_full = value_rows.astype(jnp.float32)

    def one_block(carry, block_index):
        key_sum, value_sum = carry
        start = (block_index * row_block).astype(jnp.int32)
        query_part = lax.dynamic_slice_in_dim(query3, start, row_block, 0)
        grad_part = lax.dynamic_slice_in_dim(grad3, start, row_block, 0)
        dot_part = lax.dynamic_slice_in_dim(grad_dot, start, row_block, 1)
        norm_part = lax.dynamic_slice_in_dim(log_normalizer, start, row_block, 1)
        query_pos = lax.dynamic_slice_in_dim(positions, start, row_block, 0)
        scores = jnp.einsum("ihd,jd->hij", query_part, key_full) * scaling
        allowed = positions[None, :] <= query_pos[:, None]
        probs = jnp.where(allowed[None], jnp.exp(scores - norm_part[:, :, None]), 0.0)
        grad_probs = jnp.einsum("ihd,jd->hij", grad_part, value_full)
        grad_scores = (probs * (grad_probs - dot_part[:, :, None])).astype(jnp.bfloat16)
        grad_scores = lax.optimization_barrier(grad_scores).astype(jnp.float32)
        probs_low = probs.astype(jnp.bfloat16)
        probs_low = lax.optimization_barrier(probs_low).astype(jnp.float32)
        query_grad = jnp.einsum("hij,jd->ihd", grad_scores, key_full) * scaling
        key_sum = key_sum + jnp.einsum("hij,ihd->jd", grad_scores, query_part) * scaling
        value_sum = value_sum + jnp.einsum("hij,ihd->jd", probs_low, grad_part)
        return (key_sum, value_sum), query_grad.reshape(row_block, GROUP * HD).astype(jnp.bfloat16)

    zero_rows = jnp.zeros((seq_len, HD), jnp.float32)
    (key_sum, value_sum), query_blocks = lax.scan(one_block, (zero_rows, zero_rows), jnp.arange(seq_len // row_block, dtype=jnp.int32))
    grad_query = query_blocks.reshape(seq_len, GROUP * HD)
    return grad_query, key_sum.astype(jnp.bfloat16), value_sum.astype(jnp.bfloat16)


def reference(query_rows, key_rows, value_rows, attn_output, grad_output, log_normalizer, positions):
    def per_section(operands):
        return section_grads(operands[0], operands[1], operands[2], operands[3], operands[4], operands[5], positions)

    grad_query, grad_key, grad_value = lax.map(per_section, (query_rows, key_rows, value_rows, attn_output, grad_output, log_normalizer))
    return (jnp.roll(grad_query, -1, axis=0), jnp.roll(grad_key, -1, axis=0), jnp.roll(grad_value, -1, axis=0))
```

```python
import functools
import math

import jax
import jax.numpy as jnp
from jax import lax
from jax.experimental import pallas as pl
from jax.experimental.pallas import tpu as pltpu
from jax.sharding import PartitionSpec as P

MESH = pl.DeviceIdType.MESH
LOG2E = 1.0 / math.log(2.0)
NT = (((1,), (1,)), ((), ()))
NN = (((1,), (0,)), ((), ()))
TN = (((0,), (0,)), ((), ()))


def dot(a, b, dims):
    return lax.dot_general(a, b, dims, preferred_element_type=jnp.float32)


def grid_of(ctx):
    chips = ctx // 2
    across = 1 << ((chips.bit_length() - 1) // 2)
    return chips // across, across


def kernel(
    sections, zs, xs, group,
    q_ref, k_ref, v_ref, o_ref, g_ref, norm_ref, pos_ref,
    dq_out, dk_out, dv_out,
    kv, qs, gs, rows_norm, rows_dot, dq_sum, part, part_low, core_in, x_out, x_in, z_out, z_in,
    kv_done, kv_in, dq_low,
    gz_send, gz_recv, gx_send, gx_recv, gc_send, gc_recv,
    rc_send, rc_recv, rx_send, rx_recv, rz_send, rz_recv, y_send, y_recv,
):
    rows, head = k_ref.shape
    half = rows // 2
    runs = zs * xs * 2 * 2
    scale = head ** -0.5
    s = lax.axis_index("section")
    me = lax.axis_index("ctx")
    c = lax.rem(me, 2)
    chip = lax.div(me, 2)
    x = lax.rem(chip, xs)
    z = lax.div(chip, xs)

    def shift(value, by, size):
        return lax.rem(value + (by + size), size)

    def device(zz, xx, cc):
        return (s, (zz * xs + xx) * 2 + cc)

    def z_peer(d):
        return device(shift(z, d, zs), x, c)

    def x_peer(d):
        return device(z, shift(x, d, xs), c)

    core_peer = device(z, x, 1 - c)
    before = (shift(s, -1, sections), me)
    after = (shift(s, 1, sections), me)

    def send(src, dst, send_sem, recv_sem, to):
        copy = pltpu.make_async_remote_copy(
            src_ref=src, dst_ref=dst, send_sem=send_sem, recv_sem=recv_sem,
            device_id=to, device_id_type=MESH,
        )
        return copy

    kv[chip, c, 0:rows] = k_ref[...]
    kv[chip, c, rows:2 * rows] = v_ref[...]
    run = lax.shift_right_logical(pos_ref[0:1, 0:1], half.bit_length() - 1).astype(jnp.float32)
    kv[chip, c, 2 * rows:] = jnp.broadcast_to(run, (16, head)).astype(jnp.bfloat16)

    barrier = pltpu.get_barrier_semaphore()
    peers = [z_peer(d) for d in range(1, zs)] + [x_peer(d) for d in range(1, xs)]
    peers += [core_peer, before]
    if sections > 2:
        peers.append(after)
    for peer in peers:
        pl.semaphore_signal(barrier, inc=1, device_id=peer, device_id_type=MESH)
    pl.semaphore_wait(barrier, len(peers))

    started = []

    def begin(copy):
        copy.start()
        started.append(copy)
        return copy

    def chip_at(dz, dx):
        return shift(z, -dz, zs) * xs + shift(x, -dx, xs)

    z_copies = {}
    for dz in range(1, zs):
        z_copies[dz] = begin(send(kv.at[chip, c], kv.at[chip, c], gz_send.at[dz], gz_recv.at[dz], z_peer(dz)))
    x_copies, c_copies = {}, {}

    def forward_x(dz):
        t = chip_at(dz, 0)
        for dx in range(1, xs):
            x_copies[dz, dx] = begin(send(
                kv.at[t, c], kv.at[t, c], gx_send.at[dz, dx], gx_recv.at[dz, dx], x_peer(dx)))

    def forward_c(dz, dx):
        t = chip_at(dz, dx)
        c_copies[dz, dx] = begin(send(
            kv.at[t, c], kv.at[t, c], gc_send.at[dz, dx], gc_recv.at[dz, dx], core_peer))

    forward_x(0)
    forward_c(0, 0)

    ones = jnp.ones((8, head), jnp.bfloat16)
    for h in range(group):
        cols = slice(h * head, (h + 1) * head)
        there = slice(h * rows, (h + 1) * rows)
        qs[there] = q_ref[:, cols]
        grad = g_ref[:, cols]
        gs[there] = grad
        prod = grad.astype(jnp.float32) * o_ref[:, cols].astype(jnp.float32)
        high = prod.astype(jnp.bfloat16)
        low = (prod - high.astype(jnp.float32)).astype(jnp.bfloat16)
        total = dot(ones, high, NT) + dot(ones, low, NT)
        rows_dot[:, there] = total
        rows_norm[:, there] = jnp.broadcast_to(norm_ref[h:h + 1, :] * LOG2E, (8, rows))
    dq_sum[...] = jnp.zeros_like(dq_sum)

    for dz in range(1, zs + 1):
        if dz < zs:
            z_copies[dz].wait_recv()
            forward_x(dz)
            forward_c(dz, 0)
        for dx in range(1, xs):
            x_copies[dz - 1, dx].wait_recv()
            forward_c(dz - 1, dx)
    for copy in c_copies.values():
        copy.wait_recv()

    query_pos = pos_ref[...].astype(jnp.float32)
    row_at = lax.broadcasted_iota(jnp.int32, (half, rows), 0).astype(jnp.float32)
    chunks = [(a, min(a + 2, group)) for a in range(0, group, 2)]

    def blocks(t, _):
        keys = kv[t, :, 0:rows].reshape(2 * rows, head)
        values = kv[t, :, rows:2 * rows].reshape(2 * rows, head)
        bias = []
        for core in range(2):
            first = kv[t, core, 2 * rows:].astype(jnp.float32)[0:1, :]
            low_pos = first * half + row_at
            high_pos = (runs - 1 - first) * half + row_at
            for key_pos in (low_pos, high_pos):
                bias.append(jnp.where(key_pos <= query_pos, 0.0, -1e30))
        bias = jnp.concatenate(bias, axis=0)
        dk = jnp.zeros((2 * rows, head), jnp.float32)
        dv = jnp.zeros((2 * rows, head), jnp.float32)
        for a, b in chunks:
            there = slice(a * rows, b * rows)
            query, grad = qs[there], gs[there]
            scores = dot(keys, query, NT)
            wide = jnp.concatenate([bias] * (b - a), axis=1)
            probs = jnp.exp2((scores * (scale * LOG2E) - rows_norm[0:1, there]) + wide)
            dprobs = dot(values, grad, NT)
            dscores = (probs * (dprobs - rows_dot[0:1, there])).astype(jnp.bfloat16)
            dv = dv + dot(probs.astype(jnp.bfloat16), grad, NN)
            dk = dk + dot(dscores, query, NN)
            dq_sum[there] += dot(dscores, keys, TN)
        dk = dk * scale
        for core in range(2):
            these = slice(core * rows, (core + 1) * rows)
            part[t, core, 0:rows] = dk[these]
            part[t, core, rows:] = dv[these]
            part_low[t, core, 0:rows] = dk[these].astype(jnp.bfloat16)
            part_low[t, core, rows:] = dv[these].astype(jnp.bfloat16)
        return 0

    lax.fori_loop(0, zs * xs, blocks, 0)

    core_copies = {}
    order = [zs - 1 - i for i in range(zs)]
    for dz in order:
        for dx in range(xs):
            t = chip_at(-dz, -dx)
            core_copies[dz, dx] = begin(send(
                part_low.at[t, 1 - c], core_in.at[t], rc_send.at[dz, dx], rc_recv.at[dz, dx], core_peer))
    for h in range(group):
        dq_low[:, h * head:(h + 1) * head] = (
            dq_sum[h * rows:(h + 1) * rows] * scale).astype(jnp.bfloat16)
    dq_copy = begin(send(dq_low, dq_out, y_send.at[0], y_recv.at[0], before))

    rx_copies = {}
    for dz in order:
        for dx in range(xs - 1, -1, -1):
            core_copies[dz, dx].wait_recv()
            t = chip_at(-dz, -dx)
            total = part[t, c] + core_in[t].astype(jnp.float32)
            if dx:
                x_out[dz, dx] = total.astype(jnp.bfloat16)
                rx_copies[dz, dx] = begin(send(
                    x_out.at[dz, dx], x_in.at[dz, dx], rx_send.at[dz, dx], rx_recv.at[dz, dx], x_peer(dx)))
            else:
                part[t, c] = total
    rz_copies = {}
    for dz in order:
        total = part[chip_at(-dz, 0), c]
        for dx in range(1, xs):
            rx_copies[dz, dx].wait_recv()
            total = total + x_in[dz, dx].astype(jnp.float32)
        if dz:
            z_out[dz] = total.astype(jnp.bfloat16)
            rz_copies[dz] = begin(send(
                z_out.at[dz], z_in.at[dz], rz_send.at[dz], rz_recv.at[dz], z_peer(dz)))
    for dz in range(1, zs):
        rz_copies[dz].wait_recv()
        total = total + z_in[dz].astype(jnp.float32)
    kv_done[...] = total.astype(jnp.bfloat16)
    kv_copy = begin(send(kv_done, kv_in, y_send.at[1], y_recv.at[1], before))
    kv_copy.wait_recv()
    dk_out[...] = kv_in[0:rows]
    dv_out[...] = kv_in[rows:]
    dq_copy.wait_recv()
    for copy in started:
        copy.wait_send()


def solution(mesh):
    sections = mesh.shape["section"]
    zs, xs = grid_of(mesh.shape["ctx"])

    def shards(query_rows, key_rows, value_rows, attn_output, grad_output, log_normalizer, positions):
        rows, head = key_rows.shape[1:]
        wide = query_rows.shape[2]
        group = wide // head
        chips = zs * xs
        bf16, f32 = jnp.bfloat16, jnp.float32
        dma = pltpu.SemaphoreType.DMA
        vmem = pl.BlockSpec(memory_space=pltpu.VMEM)
        dq, dk, dv = pl.pallas_call(
            functools.partial(kernel, sections, zs, xs, group),
            out_shape=(
                jax.ShapeDtypeStruct((rows, wide), bf16),
                jax.ShapeDtypeStruct((rows, head), bf16),
                jax.ShapeDtypeStruct((rows, head), bf16),
            ),
            in_specs=[vmem] * 7,
            out_specs=(vmem,) * 3,
            scratch_shapes=[
                pltpu.VMEM((chips, 2, 2 * rows + 16, head), bf16),
                pltpu.VMEM((group * rows, head), bf16),
                pltpu.VMEM((group * rows, head), bf16),
                pltpu.VMEM((8, group * rows), f32),
                pltpu.VMEM((8, group * rows), f32),
                pltpu.VMEM((group * rows, head), f32),
                pltpu.VMEM((chips, 2, 2 * rows, head), f32),
                pltpu.VMEM((chips, 2, 2 * rows, head), bf16),
                pltpu.VMEM((chips, 2 * rows, head), bf16),
                pltpu.VMEM((zs, xs, 2 * rows, head), bf16),
                pltpu.VMEM((zs, xs, 2 * rows, head), bf16),
                pltpu.VMEM((zs, 2 * rows, head), bf16),
                pltpu.VMEM((zs, 2 * rows, head), bf16),
                pltpu.VMEM((2 * rows, head), bf16),
                pltpu.VMEM((2 * rows, head), bf16),
                pltpu.VMEM((rows, wide), bf16),
                dma((zs,)), dma((zs,)),
                dma((zs, xs)), dma((zs, xs)),
                dma((zs, xs)), dma((zs, xs)),
                dma((zs, xs)), dma((zs, xs)),
                dma((zs, xs)), dma((zs, xs)),
                dma((zs,)), dma((zs,)),
                dma((2,)), dma((2,)),
            ],
            compiler_params=pltpu.CompilerParams(
                collective_id=0, has_side_effects=True, vmem_limit_bytes=48 * 1024 * 1024
            ),
        )(
            query_rows[0], key_rows[0], value_rows[0], attn_output[0], grad_output[0],
            log_normalizer[0], positions.reshape(1, rows),
        )
        return dq[None], dk[None], dv[None]

    return jax.shard_map(
        shards,
        mesh=mesh,
        in_specs=(
            P("section", "ctx", None),
            P("section", "ctx", None),
            P("section", "ctx", None),
            P("section", "ctx", None),
            P("section", "ctx", None),
            P("section", None, "ctx"),
            P("ctx"),
        ),
        out_specs=(P("section", "ctx", None),) * 3,
        check_vma=False,
    )
```

```python
import functools
import math

import jax
import jax.numpy as jnp
from jax import lax
from jax.experimental import pallas as pl
from jax.experimental.pallas import tpu as pltpu
from jax.sharding import PartitionSpec as P

MESH = pl.DeviceIdType.MESH
LOG2E = 1.0 / math.log(2.0)
NT = (((1,), (1,)), ((), ()))
NN = (((1,), (0,)), ((), ()))
TN = (((0,), (0,)), ((), ()))


def dot(a, b, dims):
    return lax.dot_general(a, b, dims, preferred_element_type=jnp.float32)


def grid_of(ctx):
    chips = ctx // 2
    across = 1 << ((chips.bit_length() - 1) // 2)
    return chips // across, across


def kernel(
    sections, zs, xs, group,
    q_hbm, k_hbm, v_hbm, o_hbm, g_hbm, norm_hbm, pos_hbm,
    dq_out, dk_out, dv_out,
    kv, qs, gs, rows_norm, rows_dot, dq_sum, part, part_low, core_in, x_out, x_in, z_out, z_in,
    kv_done, kv_in, dq_low, q_ref, o_ref, g_ref, norm_ref, pos_ref,
    gz_send, gz_recv, gx_send, gx_recv, gc_send, gc_recv,
    rc_send, rc_recv, rx_send, rx_recv, rz_send, rz_recv, y_send, y_recv, load_sem,
):
    rows, head = k_hbm.shape
    half = rows // 2
    chips = zs * xs
    runs = chips * 2 * 2
    scale = head ** -0.5
    s = lax.axis_index("section")
    me = lax.axis_index("ctx")
    c = lax.rem(me, 2)
    chip = lax.div(me, 2)
    x = lax.rem(chip, xs)
    z = lax.div(chip, xs)

    def shift(value, by, size):
        return lax.rem(value + (by + size), size)

    def device(zz, xx, cc):
        return (s, (zz * xs + xx) * 2 + cc)

    def z_peer(d):
        return device(shift(z, d, zs), x, c)

    def x_peer(d):
        return device(z, shift(x, d, xs), c)

    core_peer = device(z, x, 1 - c)
    before = (shift(s, -1, sections), me)
    after = (shift(s, 1, sections), me)

    barrier = pltpu.get_barrier_semaphore()
    peers = [z_peer(d) for d in range(1, zs)] + [x_peer(d) for d in range(1, xs)]
    peers += [core_peer, before]
    if sections > 2:
        peers.append(after)
    for peer in peers:
        pl.semaphore_signal(barrier, inc=1, device_id=peer, device_id_type=MESH)

    pairs = [
        (pos_hbm, pos_ref), (k_hbm, kv.at[chip, c, pl.ds(0, rows)]), (v_hbm, kv.at[chip, c, pl.ds(rows, rows)]),
        (q_hbm, q_ref), (g_hbm, g_ref), (o_hbm, o_ref), (norm_hbm, norm_ref),
    ]
    loads = [pltpu.make_async_copy(src, dst, load_sem.at[i]) for i, (src, dst) in enumerate(pairs)]
    for load in loads:
        load.start()
    for load in loads[:3]:
        load.wait()
    run = lax.shift_right_logical(pos_ref[0:1, 0:1], half.bit_length() - 1).astype(jnp.float32)
    kv[chip, c, 2 * rows:] = jnp.broadcast_to(run, (16, head)).astype(jnp.bfloat16)
    pl.semaphore_wait(barrier, len(peers))

    def copy_to(src, dst, send_sem, recv_sem, to):
        return pltpu.make_async_remote_copy(
            src_ref=src, dst_ref=dst, send_sem=send_sem, recv_sem=recv_sem,
            device_id=to, device_id_type=MESH,
        )

    def source(dz, dx):
        return shift(z, -dz, zs) * xs + shift(x, -dx, xs)

    def target(dz, dx):
        return shift(z, dz, zs) * xs + shift(x, dx, xs)

    def gather_z(dz):
        return copy_to(kv.at[chip, c], kv.at[chip, c], gz_send.at[dz], gz_recv.at[dz], z_peer(dz))

    def gather_x(dz, dx):
        t = source(dz, 0)
        return copy_to(kv.at[t, c], kv.at[t, c], gx_send.at[dz, dx], gx_recv.at[dz, dx], x_peer(dx))

    def gather_c(dz, dx):
        t = source(dz, dx)
        return copy_to(kv.at[t, c], kv.at[t, c], gc_send.at[dz, dx], gc_recv.at[dz, dx], core_peer)

    def pass_on(dz):
        for dx in range(1, xs):
            gather_x(dz, dx).start()
        gather_c(dz, 0).start()

    def z_service(dz):
        gather_z(dz).wait_recv()
        pass_on(dz)

    def x_service(dz):
        for dx in range(1, xs):
            gather_x(dz, dx).wait_recv()
            gather_c(dz, dx).start()

    def reduce_c(dz, dx):
        t = source(dz, dx)
        return copy_to(part_low.at[t, 1 - c], core_in.at[t], rc_send.at[dz, dx], rc_recv.at[dz, dx], core_peer)

    def reduce_x(dz, dx):
        return copy_to(x_out.at[dz, dx], x_in.at[dz, dx], rx_send.at[dz, dx], rx_recv.at[dz, dx], x_peer(-dx))

    def reduce_z(dz):
        return copy_to(z_out.at[dz], z_in.at[dz], rz_send.at[dz], rz_recv.at[dz], z_peer(-dz))

    for dz in range(1, zs):
        gather_z(dz).start()
    pass_on(0)

    for load in loads[3:]:
        load.wait()
    ones = jnp.ones((8, head), jnp.bfloat16)
    for h in range(group):
        cols = slice(h * head, (h + 1) * head)
        there = slice(h * rows, (h + 1) * rows)
        qs[there] = q_ref[:, cols]
        grad = g_ref[:, cols]
        gs[there] = grad
        prod = grad.astype(jnp.float32) * o_ref[:, cols].astype(jnp.float32)
        high = prod.astype(jnp.bfloat16)
        low = (prod - high.astype(jnp.float32)).astype(jnp.bfloat16)
        total = dot(ones, high, NT) + dot(ones, low, NT)
        rows_dot[:, there] = total
        rows_norm[:, there] = jnp.broadcast_to(norm_ref[h] * LOG2E, (8, rows))
    dq_sum[...] = jnp.zeros_like(dq_sum)
    x_service(0)
    z_service(1)

    query_pos = pos_ref[...].astype(jnp.float32)
    row_at = lax.broadcasted_iota(jnp.int32, (half, rows), 0).astype(jnp.float32)
    chunks = [(a, min(a + 2, group)) for a in range(0, group, 2)]

    def tile(t):
        keys = kv[t, :, 0:rows].reshape(2 * rows, head)
        values = kv[t, :, rows:2 * rows].reshape(2 * rows, head)
        bias = []
        for core in range(2):
            first = kv[t, core, 2 * rows:].astype(jnp.float32)[0:1, :]
            low_pos = first * half + row_at
            high_pos = (runs - 1 - first) * half + row_at
            for key_pos in (low_pos, high_pos):
                bias.append(jnp.where(key_pos <= query_pos, 0.0, -1e30))
        bias = jnp.concatenate(bias, axis=0)
        dk = jnp.zeros((2 * rows, head), jnp.float32)
        dv = jnp.zeros((2 * rows, head), jnp.float32)
        for a, b in chunks:
            there = slice(a * rows, b * rows)
            query, grad = qs[there], gs[there]
            scores = dot(keys, query, NT)
            wide = jnp.concatenate([bias] * (b - a), axis=1)
            probs = jnp.exp2((scores * (scale * LOG2E) - rows_norm[0:1, there]) + wide)
            dprobs = dot(values, grad, NT)
            dscores = (probs * (dprobs - rows_dot[0:1, there])).astype(jnp.bfloat16)
            dv = dv + dot(probs.astype(jnp.bfloat16), grad, NN)
            dk = dk + dot(dscores, query, NN)
            dq_sum[there] += dot(dscores, keys, TN)
        dk = dk * scale
        for core in range(2):
            these = slice(core * rows, (core + 1) * rows)
            part[t, core, 0:rows] = dk[these]
            part[t, core, rows:] = dv[these]
            part_low[t, core, 0:rows] = dk[these].astype(jnp.bfloat16)
            part_low[t, core, rows:] = dv[these].astype(jnp.bfloat16)

    def place(j):
        at = lax.rem(j + 1, chips)
        dz = lax.div(at, xs)
        r = lax.rem(at, xs)
        far = lax.div(dz + (zs - 1), zs)
        return dz, r + far * (xs - 1 - 2 * r), r

    def core_total(dz, dx):
        t = source(dz, dx)
        reduce_c(dz, dx).wait_recv()
        return part[t, c] + core_in[t].astype(jnp.float32)

    def row_total(dz, total):
        for dx in range(1, xs):
            reduce_x(dz, dx).wait_recv()
            total = total + x_in[dz, dx].astype(jnp.float32)
        return total

    def after_core(dz, dx):
        total = core_total(dz, dx)

        @pl.when(dx > 0)
        def _():
            x_out[dz, dx] = total.astype(jnp.bfloat16)
            reduce_x(dz, dx).start()

        @pl.when(dx == 0)
        def _():
            part[source(dz, 0), c] = total

    def after_row(dz):
        z_out[dz] = row_total(dz, part[source(dz, 0), c]).astype(jnp.bfloat16)
        reduce_z(dz).start()

    def step(j, _):
        dz, dx, r = place(j)
        row_start = jnp.logical_and(jnp.logical_and(r == 0, dz > 0), dz < zs - 1)

        @pl.when(row_start)
        def _():
            z_service(dz + 1)

        gather_c(dz, dx).wait_recv()
        tile(source(dz, dx))
        reduce_c(dz, dx).start()

        @pl.when(jnp.logical_or(row_start, j == xs - 2))
        def _():
            x_service(dz + 1)

        @pl.when(j > 0)
        def _():
            dz1, dx1, _r = place(j - 1)
            after_core(dz1, dx1)

        @pl.when(j > 1)
        def _():
            dz2, dx2, _r = place(j - 2)

            @pl.when(jnp.logical_and(dz2 > 0, dx2 == 0))
            def _():
                after_row(dz2)

        return 0

    lax.fori_loop(0, chips, step, 0)

    for h in range(group):
        dq_low[:, h * head:(h + 1) * head] = (
            dq_sum[h * rows:(h + 1) * rows] * scale).astype(jnp.bfloat16)
    dq_copy = copy_to(dq_low, dq_out, y_send.at[0], y_recv.at[0], before)
    dq_copy.start()
    after_row(zs - 1)
    total = row_total(0, core_total(0, 0))
    for dz in range(1, zs):
        reduce_z(dz).wait_recv()
        total = total + z_in[dz].astype(jnp.float32)
    kv_done[...] = total.astype(jnp.bfloat16)
    kv_copy = copy_to(kv_done, kv_in, y_send.at[1], y_recv.at[1], before)
    kv_copy.start()
    kv_copy.wait_recv()
    dk_out[...] = kv_in[0:rows]
    dv_out[...] = kv_in[rows:]
    dq_copy.wait_recv()
    dq_copy.wait_send()
    kv_copy.wait_send()
    for dz in range(zs):
        if dz:
            gather_z(dz).wait_send()
            reduce_z(dz).wait_send()
        for dx in range(xs):
            if dx:
                gather_x(dz, dx).wait_send()
                reduce_x(dz, dx).wait_send()
            gather_c(dz, dx).wait_send()
            reduce_c(dz, dx).wait_send()


def solution(mesh):
    sections = mesh.shape["section"]
    zs, xs = grid_of(mesh.shape["ctx"])

    def shards(query_rows, key_rows, value_rows, attn_output, grad_output, log_normalizer, positions):
        rows, head = key_rows.shape[1:]
        wide = query_rows.shape[2]
        group = wide // head
        chips = zs * xs
        bf16, f32 = jnp.bfloat16, jnp.float32
        dma = pltpu.SemaphoreType.DMA
        vmem = pl.BlockSpec(memory_space=pltpu.VMEM)
        dq, dk, dv = pl.pallas_call(
            functools.partial(kernel, sections, zs, xs, group),
            out_shape=(
                jax.ShapeDtypeStruct((rows, wide), bf16),
                jax.ShapeDtypeStruct((rows, head), bf16),
                jax.ShapeDtypeStruct((rows, head), bf16),
            ),
            in_specs=[pl.BlockSpec(memory_space=pltpu.HBM)] * 7,
            out_specs=(vmem,) * 3,
            scratch_shapes=[
                pltpu.VMEM((chips, 2, 2 * rows + 16, head), bf16),
                pltpu.VMEM((group * rows, head), bf16),
                pltpu.VMEM((group * rows, head), bf16),
                pltpu.VMEM((8, group * rows), f32),
                pltpu.VMEM((8, group * rows), f32),
                pltpu.VMEM((group * rows, head), f32),
                pltpu.VMEM((chips, 2, 2 * rows, head), f32),
                pltpu.VMEM((chips, 2, 2 * rows, head), bf16),
                pltpu.VMEM((chips, 2 * rows, head), bf16),
                pltpu.VMEM((zs, xs, 2 * rows, head), bf16),
                pltpu.VMEM((zs, xs, 2 * rows, head), bf16),
                pltpu.VMEM((zs, 2 * rows, head), bf16),
                pltpu.VMEM((zs, 2 * rows, head), bf16),
                pltpu.VMEM((2 * rows, head), bf16),
                pltpu.VMEM((2 * rows, head), bf16),
                pltpu.VMEM((rows, wide), bf16),
                pltpu.VMEM((rows, wide), bf16),
                pltpu.VMEM((rows, wide), bf16),
                pltpu.VMEM((rows, wide), bf16),
                pltpu.VMEM((group, 1, rows), f32),
                pltpu.VMEM((1, rows), jnp.int32),
                dma((zs,)), dma((zs,)),
                dma((zs, xs)), dma((zs, xs)),
                dma((zs, xs)), dma((zs, xs)),
                dma((zs, xs)), dma((zs, xs)),
                dma((zs, xs)), dma((zs, xs)),
                dma((zs,)), dma((zs,)),
                dma((2,)), dma((2,)), dma((7,)),
            ],
            compiler_params=pltpu.CompilerParams(
                collective_id=0, has_side_effects=True, vmem_limit_bytes=63 * 1024 * 1024
            ),
        )(
            query_rows[0], key_rows[0], value_rows[0], attn_output[0], grad_output[0],
            log_normalizer.transpose(1, 0, 2), positions.reshape(1, rows),
        )
        return dq[None], dk[None], dv[None]

    return jax.shard_map(
        shards,
        mesh=mesh,
        in_specs=(
            P("section", "ctx", None),
            P("section", "ctx", None),
            P("section", "ctx", None),
            P("section", "ctx", None),
            P("section", "ctx", None),
            P("section", None, "ctx"),
            P("ctx"),
        ),
        out_specs=(P("section", "ctx", None),) * 3,
        check_vma=False,
    )
```

```python
import functools
import math

import jax
import jax.numpy as jnp
from jax import lax
from jax.experimental import pallas as pl
from jax.experimental.pallas import tpu as pltpu
from jax.sharding import PartitionSpec as P

MESH = pl.DeviceIdType.MESH
LOG2E = 1.0 / math.log(2.0)
NT = (((1,), (1,)), ((), ()))
NN = (((1,), (0,)), ((), ()))
TN = (((0,), (0,)), ((), ()))


def dot(a, b, dims):
    return lax.dot_general(a, b, dims, preferred_element_type=jnp.float32)


def grid_of(ctx):
    chips = ctx // 2
    across = 1 << ((chips.bit_length() - 1) // 2)
    return chips // across, across


def kernel(
    sections, zs, xs, group,
    q_hbm, k_hbm, v_hbm, o_hbm, g_hbm, norm_hbm, pos_hbm,
    dq_out, dk_out, dv_out,
    kv, qs, gs, rows_norm, rows_dot, dq_sum, part, part_low, core_in, x_out, x_in,
    kv_done, dq_low, q_ref, o_ref, g_ref, norm_ref, pos_ref,
    gz_send, gz_recv, gx_send, gx_recv, gc_send, gc_recv,
    rc_send, rc_recv, rx_send, rx_recv, y_send, y_recv, load_sem,
):
    rows, head = k_hbm.shape
    half = rows // 2
    chips = zs * xs
    runs = chips * 2 * 2
    scale = head ** -0.5
    s = lax.axis_index("section")
    me = lax.axis_index("ctx")
    c = lax.rem(me, 2)
    chip = lax.div(me, 2)
    x = lax.rem(chip, xs)
    z = lax.div(chip, xs)

    def shift(value, by, size):
        return lax.rem(value + (by + size), size)

    def device(zz, xx, cc):
        return (s, (zz * xs + xx) * 2 + cc)

    def z_peer(d):
        return device(shift(z, d, zs), x, c)

    def x_peer(d):
        return device(z, shift(x, d, xs), c)

    def direct(dz, dx):
        return device(shift(z, dz, zs), shift(x, dx, xs), c)

    core_peer = device(z, x, 1 - c)
    before = (shift(s, -1, sections), me)
    after = (shift(s, 1, sections), me)

    barrier = pltpu.get_barrier_semaphore()
    peers = [direct(dz, dx) for dz in range(zs) for dx in range(xs) if dz or dx]
    peers += [core_peer, before]
    if sections > 2:
        peers.append(after)
    for peer in peers:
        pl.semaphore_signal(barrier, inc=1, device_id=peer, device_id_type=MESH)

    pairs = [
        (pos_hbm, pos_ref), (k_hbm, kv.at[chip, c, pl.ds(0, rows)]), (v_hbm, kv.at[chip, c, pl.ds(rows, rows)]),
        (q_hbm, q_ref), (g_hbm, g_ref), (o_hbm, o_ref), (norm_hbm, norm_ref),
    ]
    loads = [pltpu.make_async_copy(src, dst, load_sem.at[i]) for i, (src, dst) in enumerate(pairs)]
    for load in loads:
        load.start()
    for load in loads[:3]:
        load.wait()
    run = lax.shift_right_logical(pos_ref[0:1, 0:1], half.bit_length() - 1).astype(jnp.float32)
    kv[chip, c, 2 * rows:] = jnp.broadcast_to(run, (16, head)).astype(jnp.bfloat16)
    pl.semaphore_wait(barrier, len(peers))

    def copy_to(src, dst, send_sem, recv_sem, to):
        return pltpu.make_async_remote_copy(
            src_ref=src, dst_ref=dst, send_sem=send_sem, recv_sem=recv_sem,
            device_id=to, device_id_type=MESH,
        )

    def source(dz, dx):
        return shift(z, -dz, zs) * xs + shift(x, -dx, xs)

    def target(dz, dx):
        return shift(z, dz, zs) * xs + shift(x, dx, xs)

    def gather_z(dz):
        return copy_to(kv.at[chip, c], kv.at[chip, c], gz_send.at[dz], gz_recv.at[dz], z_peer(dz))

    def gather_x(dz, dx):
        t = source(dz, 0)
        return copy_to(kv.at[t, c], kv.at[t, c], gx_send.at[dz, dx], gx_recv.at[dz, dx], x_peer(dx))

    def gather_c(dz, dx):
        t = source(dz, dx)
        return copy_to(kv.at[t, c], kv.at[t, c], gc_send.at[dz, dx], gc_recv.at[dz, dx], core_peer)

    def pass_on(dz):
        for dx in range(1, xs):
            gather_x(dz, dx).start()
        gather_c(dz, 0).start()

    def z_service(dz):
        gather_z(dz).wait_recv()
        pass_on(dz)

    def x_service(dz):
        for dx in range(1, xs):
            gather_x(dz, dx).wait_recv()
            gather_c(dz, dx).start()

    def reduce_c(dz, dx):
        t = source(dz, dx)
        return copy_to(part_low.at[t, 1 - c], core_in.at[t], rc_send.at[dz, dx], rc_recv.at[dz, dx], core_peer)

    def reduce_x(dz, dx):
        return copy_to(x_out.at[dz, dx], x_in.at[dz, dx], rx_send.at[dz, dx], rx_recv.at[dz, dx], direct(-dz, -dx))

    for dz in range(1, zs):
        gather_z(dz).start()
    pass_on(0)

    for load in loads[3:]:
        load.wait()
    ones = jnp.ones((8, head), jnp.bfloat16)
    for h in range(group):
        cols = slice(h * head, (h + 1) * head)
        there = slice(h * rows, (h + 1) * rows)
        qs[there] = q_ref[:, cols]
        grad = g_ref[:, cols]
        gs[there] = grad
        prod = grad.astype(jnp.float32) * o_ref[:, cols].astype(jnp.float32)
        high = prod.astype(jnp.bfloat16)
        low = (prod - high.astype(jnp.float32)).astype(jnp.bfloat16)
        total = dot(ones, high, NT) + dot(ones, low, NT)
        rows_dot[:, there] = total
        rows_norm[:, there] = jnp.broadcast_to(norm_ref[h] * LOG2E, (8, rows))
    dq_sum[...] = jnp.zeros_like(dq_sum)
    x_service(0)
    z_service(1)

    query_pos = pos_ref[...].astype(jnp.float32)
    row_at = lax.broadcasted_iota(jnp.int32, (half, rows), 0).astype(jnp.float32)
    chunks = [(a, min(a + 2, group)) for a in range(0, group, 2)]

    def tile(t):
        keys = kv[t, :, 0:rows].reshape(2 * rows, head)
        values = kv[t, :, rows:2 * rows].reshape(2 * rows, head)
        bias = []
        for core in range(2):
            first = kv[t, core, 2 * rows:].astype(jnp.float32)[0:1, :]
            low_pos = first * half + row_at
            high_pos = (runs - 1 - first) * half + row_at
            for key_pos in (low_pos, high_pos):
                bias.append(jnp.where(key_pos <= query_pos, 0.0, -1e30))
        bias = jnp.concatenate(bias, axis=0)
        dk = jnp.zeros((2 * rows, head), jnp.float32)
        dv = jnp.zeros((2 * rows, head), jnp.float32)
        for a, b in chunks:
            there = slice(a * rows, b * rows)
            query, grad = qs[there], gs[there]
            scores = dot(keys, query, NT)
            wide = jnp.concatenate([bias] * (b - a), axis=1)
            probs = jnp.exp2((scores * (scale * LOG2E) - rows_norm[0:1, there]) + wide)
            dprobs = dot(values, grad, NT)
            dscores = (probs * (dprobs - rows_dot[0:1, there])).astype(jnp.bfloat16)
            dv = dv + dot(probs.astype(jnp.bfloat16), grad, NN)
            dk = dk + dot(dscores, query, NN)
            dq_sum[there] += dot(dscores, keys, TN)
        dk = dk * scale
        for core in range(2):
            these = slice(core * rows, (core + 1) * rows)
            part[t, core, 0:rows] = dk[these]
            part[t, core, rows:] = dv[these]
            part_low[t, core, 0:rows] = dk[these].astype(jnp.bfloat16)
            part_low[t, core, rows:] = dv[these].astype(jnp.bfloat16)

    def place(j):
        at = lax.rem(j + 1, chips)
        dz = lax.div(at, xs)
        r = lax.rem(at, xs)
        last = lax.div(dz, zs - 1)
        return dz, r + last * (xs - 1 - 2 * r), r

    def core_total(dz, dx):
        t = source(dz, dx)
        reduce_c(dz, dx).wait_recv()
        return part[t, c] + core_in[t].astype(jnp.float32)

    def after_core(dz, dx):
        x_out[dz, dx] = core_total(dz, dx).astype(jnp.bfloat16)
        reduce_x(dz, dx).start()

    def step(j, _):
        dz, dx, r = place(j)
        gather_c(dz, dx).wait_recv()
        tile(source(dz, dx))
        reduce_c(dz, dx).start()

        @pl.when(j == xs - 2)
        def _():
            z_service(2)

        @pl.when(jnp.logical_and(r == 0, jnp.logical_and(dz > 0, dz < zs - 2)))
        def _():
            z_service(dz + 2)

        @pl.when(jnp.logical_and(r == xs - 1, dz < zs - 2))
        def _():
            x_service(dz + 1)

        @pl.when(jnp.logical_and(r == 0, dz == zs - 2))
        def _():
            x_service(dz + 1)

        @pl.when(j > 1)
        def _():
            dz2, dx2, _r = place(j - 2)
            after_core(dz2, dx2)

        return 0

    lax.fori_loop(0, chips, step, 0)

    for h in range(group):
        dq_low[:, h * head:(h + 1) * head] = (
            dq_sum[h * rows:(h + 1) * rows] * scale).astype(jnp.bfloat16)
    dq_copy = copy_to(dq_low, dq_out, y_send.at[0], y_recv.at[0], before)
    dq_copy.start()
    after_core(zs - 1, 0)
    total = core_total(0, 0)
    for dz in range(zs):
        for dx in range(xs):
            if dz or dx:
                reduce_x(dz, dx).wait_recv()
                total = total + x_in[dz, dx].astype(jnp.float32)
    kv_done[...] = total.astype(jnp.bfloat16)
    dk_copy = copy_to(kv_done.at[pl.ds(0, rows)], dk_out, y_send.at[1], y_recv.at[1], before)
    dv_copy = copy_to(kv_done.at[pl.ds(rows, rows)], dv_out, y_send.at[2], y_recv.at[2], before)
    dk_copy.start()
    dv_copy.start()
    for copy in (dq_copy, dk_copy, dv_copy):
        copy.wait_recv()
        copy.wait_send()
    for dz in range(zs):
        if dz:
            gather_z(dz).wait_send()
        for dx in range(xs):
            if dx:
                gather_x(dz, dx).wait_send()
            gather_c(dz, dx).wait_send()
            reduce_c(dz, dx).wait_send()
            if dz or dx:
                reduce_x(dz, dx).wait_send()


def finish(dq, dk, dv, dq_out, dk_out, dv_out):
    dq_out[...] = dq[...]
    dk_out[...] = dk[...]
    dv_out[...] = dv[...]


def solution(mesh):
    sections = mesh.shape["section"]
    zs, xs = grid_of(mesh.shape["ctx"])

    def shards(query_rows, key_rows, value_rows, attn_output, grad_output, log_normalizer, positions):
        rows, head = key_rows.shape[1:]
        wide = query_rows.shape[2]
        group = wide // head
        chips = zs * xs
        bf16, f32 = jnp.bfloat16, jnp.float32
        dma = pltpu.SemaphoreType.DMA
        hbm = pl.BlockSpec(memory_space=pltpu.HBM)
        dq, dk, dv = pl.pallas_call(
            functools.partial(kernel, sections, zs, xs, group),
            out_shape=(
                jax.ShapeDtypeStruct((rows, wide), bf16),
                jax.ShapeDtypeStruct((rows, head), bf16),
                jax.ShapeDtypeStruct((rows, head), bf16),
            ),
            in_specs=[hbm] * 7,
            out_specs=(hbm,) * 3,
            scratch_shapes=[
                pltpu.VMEM((chips, 2, 2 * rows + 16, head), bf16),
                pltpu.VMEM((group * rows, head), bf16),
                pltpu.VMEM((group * rows, head), bf16),
                pltpu.VMEM((8, group * rows), f32),
                pltpu.VMEM((8, group * rows), f32),
                pltpu.VMEM((group * rows, head), f32),
                pltpu.VMEM((chips, 2, 2 * rows, head), f32),
                pltpu.VMEM((chips, 2, 2 * rows, head), bf16),
                pltpu.VMEM((chips, 2 * rows, head), bf16),
                pltpu.VMEM((zs, xs, 2 * rows, head), bf16),
                pltpu.VMEM((zs, xs, 2 * rows, head), bf16),
                pltpu.VMEM((2 * rows, head), bf16),
                pltpu.VMEM((rows, wide), bf16),
                pltpu.VMEM((rows, wide), bf16),
                pltpu.VMEM((rows, wide), bf16),
                pltpu.VMEM((rows, wide), bf16),
                pltpu.VMEM((group, 1, rows), f32),
                pltpu.VMEM((1, rows), jnp.int32),
                dma((zs,)), dma((zs,)),
                dma((zs, xs)), dma((zs, xs)),
                dma((zs, xs)), dma((zs, xs)),
                dma((zs, xs)), dma((zs, xs)),
                dma((zs, xs)), dma((zs, xs)),
                dma((3,)), dma((3,)), dma((7,)),
            ],
            compiler_params=pltpu.CompilerParams(
                collective_id=0, has_side_effects=True, vmem_limit_bytes=63 * 1024 * 1024
            ),
        )(
            query_rows[0], key_rows[0], value_rows[0], attn_output[0], grad_output[0],
            log_normalizer.transpose(1, 0, 2), positions.reshape(1, rows),
        )
        vmem = pl.BlockSpec(memory_space=pltpu.VMEM)
        dq, dk, dv = pl.pallas_call(
            finish,
            out_shape=(
                jax.ShapeDtypeStruct((rows, wide), bf16),
                jax.ShapeDtypeStruct((rows, head), bf16),
                jax.ShapeDtypeStruct((rows, head), bf16),
            ),
            in_specs=[vmem] * 3,
            out_specs=(vmem,) * 3,
        )(dq, dk, dv)
        return dq[None], dk[None], dv[None]

    return jax.shard_map(
        shards,
        mesh=mesh,
        in_specs=(
            P("section", "ctx", None),
            P("section", "ctx", None),
            P("section", "ctx", None),
            P("section", "ctx", None),
            P("section", "ctx", None),
            P("section", None, "ctx"),
            P("ctx"),
        ),
        out_specs=(P("section", "ctx", None),) * 3,
        check_vma=False,
    )
```

```python
import functools
import math

import jax
import jax.numpy as jnp
from jax import lax
from jax.experimental import pallas as pl
from jax.experimental.pallas import tpu as pltpu
from jax.sharding import PartitionSpec as P

MESH = pl.DeviceIdType.MESH
LOG2E = 1.0 / math.log(2.0)
NT = (((1,), (1,)), ((), ()))
NN = (((1,), (0,)), ((), ()))
TN = (((0,), (0,)), ((), ()))


def dot(a, b, dims):
    return lax.dot_general(a, b, dims, preferred_element_type=jnp.float32)


def grid_of(ctx):
    chips = ctx // 2
    across = 1 << ((chips.bit_length() - 1) // 2)
    return chips // across, across


def kernel(
    sections, zs, xs, group,
    q_hbm, k_hbm, v_hbm, o_hbm, g_hbm, norm_hbm, pos_hbm,
    dq_out, dk_out, dv_out,
    kv, qs, gs, rows_norm, rows_dot, dq_sum, part, part_low, core_in, x_out, x_in,
    kv_done, dq_low, q_ref, o_ref, g_ref, norm_ref, pos_ref,
    gz_send, gz_recv, gx_send, gx_recv, gc_send, gc_recv,
    rc_send, rc_recv, rx_send, rx_recv, y_send, y_recv, load_sem,
):
    rows, head = k_hbm.shape
    half = rows // 2
    chips = zs * xs
    runs = chips * 2 * 2
    scale = head ** -0.5
    s = lax.axis_index("section")
    me = lax.axis_index("ctx")
    c = lax.rem(me, 2)
    chip = lax.div(me, 2)
    x = lax.rem(chip, xs)
    z = lax.div(chip, xs)

    def shift(value, by, size):
        return lax.rem(value + (by + size), size)

    def device(zz, xx, cc):
        return (s, (zz * xs + xx) * 2 + cc)

    def z_peer(d):
        return device(shift(z, d, zs), x, c)

    def x_peer(d):
        return device(z, shift(x, d, xs), c)

    def direct(dz, dx):
        return device(shift(z, dz, zs), shift(x, dx, xs), c)

    core_peer = device(z, x, 1 - c)
    before = (shift(s, -1, sections), me)
    after = (shift(s, 1, sections), me)

    barrier = pltpu.get_barrier_semaphore()
    peers = [direct(dz, dx) for dz in range(zs) for dx in range(xs) if dz or dx]
    peers += [core_peer, before]
    if sections > 2:
        peers.append(after)
    for peer in peers:
        pl.semaphore_signal(barrier, inc=1, device_id=peer, device_id_type=MESH)

    pairs = [
        (pos_hbm, pos_ref), (k_hbm, kv.at[chip, c, pl.ds(0, rows)]), (v_hbm, kv.at[chip, c, pl.ds(rows, rows)]),
        (q_hbm, q_ref), (g_hbm, g_ref), (o_hbm, o_ref), (norm_hbm, norm_ref),
    ]
    loads = [pltpu.make_async_copy(src, dst, load_sem.at[i]) for i, (src, dst) in enumerate(pairs)]
    for load in loads:
        load.start()
    for load in loads[:3]:
        load.wait()
    run = lax.shift_right_logical(pos_ref[0:1, 0:1], half.bit_length() - 1).astype(jnp.float32)
    kv[chip, c, 2 * rows:] = jnp.broadcast_to(run, (16, head)).astype(jnp.bfloat16)
    pl.semaphore_wait(barrier, len(peers))

    def copy_to(src, dst, send_sem, recv_sem, to):
        return pltpu.make_async_remote_copy(
            src_ref=src, dst_ref=dst, send_sem=send_sem, recv_sem=recv_sem,
            device_id=to, device_id_type=MESH,
        )

    def source(dz, dx):
        return shift(z, -dz, zs) * xs + shift(x, -dx, xs)

    def target(dz, dx):
        return shift(z, dz, zs) * xs + shift(x, dx, xs)

    def gather_z(dz):
        return copy_to(kv.at[chip, c], kv.at[chip, c], gz_send.at[dz], gz_recv.at[dz], z_peer(dz))

    def gather_x(dz, dx):
        t = source(dz, 0)
        return copy_to(kv.at[t, c], kv.at[t, c], gx_send.at[dz, dx], gx_recv.at[dz, dx], x_peer(dx))

    def gather_c(dz, dx):
        t = source(dz, dx)
        return copy_to(kv.at[t, c], kv.at[t, c], gc_send.at[dz, dx], gc_recv.at[dz, dx], core_peer)

    def pass_on(dz):
        for dx in range(1, xs):
            gather_x(dz, dx).start()
        gather_c(dz, 0).start()

    def z_service(dz):
        gather_z(dz).wait_recv()
        pass_on(dz)

    def x_service(dz):
        for dx in range(1, xs):
            gather_x(dz, dx).wait_recv()
            gather_c(dz, dx).start()

    def reduce_c(dz, dx):
        t = source(dz, dx)
        return copy_to(part_low.at[t, 1 - c], core_in.at[t], rc_send.at[dz, dx], rc_recv.at[dz, dx], core_peer)

    def reduce_x(dz, dx):
        return copy_to(x_out.at[dz, dx], x_in.at[dz, dx], rx_send.at[dz, dx], rx_recv.at[dz, dx], direct(-dz, -dx))

    for dz in range(1, zs):
        gather_z(dz).start()
    pass_on(0)

    for load in loads[3:]:
        load.wait()
    ones = jnp.ones((8, head), jnp.bfloat16)
    for h in range(group):
        cols = slice(h * head, (h + 1) * head)
        there = slice(h * rows, (h + 1) * rows)
        qs[there] = q_ref[:, cols]
        grad = g_ref[:, cols]
        gs[there] = grad
        prod = grad.astype(jnp.float32) * o_ref[:, cols].astype(jnp.float32)
        high = prod.astype(jnp.bfloat16)
        low = (prod - high.astype(jnp.float32)).astype(jnp.bfloat16)
        total = dot(ones, high, NT) + dot(ones, low, NT)
        rows_dot[:, there] = total
        rows_norm[:, there] = jnp.broadcast_to(norm_ref[h] * LOG2E, (8, rows))
    dq_sum[...] = jnp.zeros_like(dq_sum)
    x_service(0)
    z_service(1)

    query_pos = pos_ref[...].astype(jnp.float32)
    row_at = lax.broadcasted_iota(jnp.int32, (half, rows), 0).astype(jnp.float32)
    chunks = [(a, min(a + 2, group)) for a in range(0, group, 2)]

    def tile(t):
        keys = kv[t, :, 0:rows].reshape(2 * rows, head)
        values = kv[t, :, rows:2 * rows].reshape(2 * rows, head)
        bias = []
        for core in range(2):
            first = kv[t, core, 2 * rows:].astype(jnp.float32)[0:1, :]
            low_pos = first * half + row_at
            high_pos = (runs - 1 - first) * half + row_at
            for key_pos in (low_pos, high_pos):
                bias.append(jnp.where(key_pos <= query_pos, 0.0, -1e30))
        bias = jnp.concatenate(bias, axis=0)
        dk = jnp.zeros((2 * rows, head), jnp.float32)
        dv = jnp.zeros((2 * rows, head), jnp.float32)
        for a, b in chunks:
            there = slice(a * rows, b * rows)
            query, grad = qs[there], gs[there]
            scores = dot(keys, query, NT)
            wide = jnp.concatenate([bias] * (b - a), axis=1)
            probs = jnp.exp2((scores * (scale * LOG2E) - rows_norm[0:1, there]) + wide)
            dprobs = dot(values, grad, NT)
            dscores = (probs * (dprobs - rows_dot[0:1, there])).astype(jnp.bfloat16)
            dv = dv + dot(probs.astype(jnp.bfloat16), grad, NN)
            dk = dk + dot(dscores, query, NN)
            dq_sum[there] += dot(dscores, keys, TN)
        dk = dk * scale
        for core in range(2):
            these = slice(core * rows, (core + 1) * rows)
            part[t, core, 0:rows] = dk[these]
            part[t, core, rows:] = dv[these]
            part_low[t, core, 0:rows] = dk[these].astype(jnp.bfloat16)
            part_low[t, core, rows:] = dv[these].astype(jnp.bfloat16)

    def place(j):
        at = lax.rem(j + 1, chips)
        dz = lax.div(at, xs)
        r = lax.rem(at, xs)
        last = lax.div(dz, zs - 1)
        return dz, r + last * (xs - 1 - 2 * r), r

    def core_total(dz, dx):
        t = source(dz, dx)
        reduce_c(dz, dx).wait_recv()
        return part[t, c] + core_in[t].astype(jnp.float32)

    def after_core(dz, dx):
        x_out[dz, dx] = core_total(dz, dx).astype(jnp.bfloat16)
        reduce_x(dz, dx).start()

    def step(j, _):
        dz, dx, r = place(j)
        gather_c(dz, dx).wait_recv()
        tile(source(dz, dx))
        reduce_c(dz, dx).start()

        @pl.when(j == xs - 2)
        def _():
            z_service(2)

        @pl.when(jnp.logical_and(r == 0, jnp.logical_and(dz > 0, dz < zs - 2)))
        def _():
            z_service(dz + 2)

        @pl.when(jnp.logical_and(r == xs - 1, dz < zs - 2))
        def _():
            x_service(dz + 1)

        @pl.when(jnp.logical_and(r == 0, dz == zs - 2))
        def _():
            x_service(dz + 1)

        @pl.when(j > 0)
        def _():
            dz2, dx2, _r = place(j - 1)
            after_core(dz2, dx2)

        return 0

    lax.fori_loop(0, chips, step, 0)

    for h in range(group):
        dq_low[:, h * head:(h + 1) * head] = (
            dq_sum[h * rows:(h + 1) * rows] * scale).astype(jnp.bfloat16)
    dq_copy = copy_to(dq_low, dq_out, y_send.at[0], y_recv.at[0], before)
    dq_copy.start()
    total = core_total(0, 0)
    for dz in range(zs):
        for dx in range(xs):
            if dz or dx:
                reduce_x(dz, dx).wait_recv()
                total = total + x_in[dz, dx].astype(jnp.float32)
    kv_done[...] = total.astype(jnp.bfloat16)
    dk_copy = copy_to(kv_done.at[pl.ds(0, rows)], dk_out, y_send.at[1], y_recv.at[1], before)
    dv_copy = copy_to(kv_done.at[pl.ds(rows, rows)], dv_out, y_send.at[2], y_recv.at[2], before)
    dk_copy.start()
    dv_copy.start()
    for copy in (dq_copy, dk_copy, dv_copy):
        copy.wait_recv()
        copy.wait_send()
    for dz in range(zs):
        if dz:
            gather_z(dz).wait_send()
        for dx in range(xs):
            if dx:
                gather_x(dz, dx).wait_send()
            gather_c(dz, dx).wait_send()
            reduce_c(dz, dx).wait_send()
            if dz or dx:
                reduce_x(dz, dx).wait_send()


def finish(dq, dk, dv, dq_out, dk_out, dv_out):
    dq_out[...] = dq[...]
    dk_out[...] = dk[...]
    dv_out[...] = dv[...]


def solution(mesh):
    sections = mesh.shape["section"]
    zs, xs = grid_of(mesh.shape["ctx"])

    def shards(query_rows, key_rows, value_rows, attn_output, grad_output, log_normalizer, positions):
        rows, head = key_rows.shape[1:]
        wide = query_rows.shape[2]
        group = wide // head
        chips = zs * xs
        bf16, f32 = jnp.bfloat16, jnp.float32
        dma = pltpu.SemaphoreType.DMA
        hbm = pl.BlockSpec(memory_space=pltpu.HBM)
        dq, dk, dv = pl.pallas_call(
            functools.partial(kernel, sections, zs, xs, group),
            out_shape=(
                jax.ShapeDtypeStruct((rows, wide), bf16),
                jax.ShapeDtypeStruct((rows, head), bf16),
                jax.ShapeDtypeStruct((rows, head), bf16),
            ),
            in_specs=[hbm] * 7,
            out_specs=(hbm,) * 3,
            scratch_shapes=[
                pltpu.VMEM((chips, 2, 2 * rows + 16, head), bf16),
                pltpu.VMEM((group * rows, head), bf16),
                pltpu.VMEM((group * rows, head), bf16),
                pltpu.VMEM((8, group * rows), f32),
                pltpu.VMEM((8, group * rows), f32),
                pltpu.VMEM((group * rows, head), f32),
                pltpu.VMEM((chips, 2, 2 * rows, head), f32),
                pltpu.VMEM((chips, 2, 2 * rows, head), bf16),
                pltpu.VMEM((chips, 2 * rows, head), bf16),
                pltpu.VMEM((zs, xs, 2 * rows, head), bf16),
                pltpu.VMEM((zs, xs, 2 * rows, head), bf16),
                pltpu.VMEM((2 * rows, head), bf16),
                pltpu.VMEM((rows, wide), bf16),
                pltpu.VMEM((rows, wide), bf16),
                pltpu.VMEM((rows, wide), bf16),
                pltpu.VMEM((rows, wide), bf16),
                pltpu.VMEM((group, 1, rows), f32),
                pltpu.VMEM((1, rows), jnp.int32),
                dma((zs,)), dma((zs,)),
                dma((zs, xs)), dma((zs, xs)),
                dma((zs, xs)), dma((zs, xs)),
                dma((zs, xs)), dma((zs, xs)),
                dma((zs, xs)), dma((zs, xs)),
                dma((3,)), dma((3,)), dma((7,)),
            ],
            compiler_params=pltpu.CompilerParams(
                collective_id=0, has_side_effects=True, vmem_limit_bytes=63 * 1024 * 1024
            ),
        )(
            query_rows[0], key_rows[0], value_rows[0], attn_output[0], grad_output[0],
            log_normalizer.transpose(1, 0, 2), positions.reshape(1, rows),
        )
        vmem = pl.BlockSpec(memory_space=pltpu.VMEM)
        dq, dk, dv = pl.pallas_call(
            finish,
            out_shape=(
                jax.ShapeDtypeStruct((rows, wide), bf16),
                jax.ShapeDtypeStruct((rows, head), bf16),
                jax.ShapeDtypeStruct((rows, head), bf16),
            ),
            in_specs=[vmem] * 3,
            out_specs=(vmem,) * 3,
        )(dq, dk, dv)
        return dq[None], dk[None], dv[None]

    return jax.shard_map(
        shards,
        mesh=mesh,
        in_specs=(
            P("section", "ctx", None),
            P("section", "ctx", None),
            P("section", "ctx", None),
            P("section", "ctx", None),
            P("section", "ctx", None),
            P("section", None, "ctx"),
            P("ctx"),
        ),
        out_specs=(P("section", "ctx", None),) * 3,
        check_vma=False,
    )
```
